256 devices in a mesh: dp: 8 (over x, core), row: 4 (over y), col: 8 (over z).
Axes of the slice: x: 4, y: 4, z: 8, core: 2. Of those that a mesh axis runs over, the one named last changes fastest.
Arguments:
- grad: bfloat16 [8, 2, 8192, 1024], P('dp', None, 'row', 'col'), may hold values from -120 to 120
- momentum: float32 [8, 2, 8192, 1024], P('dp', None, 'row', 'col'), may hold values from -120 to 120
- right_factor: float32 [1024, 2, 256], P('col'), may hold values from -0.1875 to 0.1875
Outputs:
- momentum_next: float32 [8, 2, 8192, 1024], P('dp', None, 'row', 'col')
- update: bfloat16 [2, 8192, 1024], P(None, 'row', 'col')
- factor_next: float32 [1024, 2, 256], P('col')
The draws below stay inside these ranges and needn't reach their ends.
All inputs are finite; a program needn't handle non-finite values.
Results may differ from the reference program's by a relative error of at most 0.001.
Values sent between devices are 32-bit elements; how exact they have to be, the bound alone decides.
No kernel may reach another device: no remote copies, remote signals or barrier semaphores. Data moves between devices by JAX's collectives and lax.ppermute only.
A program may use at most 64 MiB of HBM per device.

```python
import math
import jax
import jax.numpy as jnp
from jax import lax

D = 8192
KV = 1024
RANK = 256
MATS = 2
ITERS = 2
REPLICAS = 8


def scale_field(key, spread):
    key_rows, key_cols = jax.random.split(key, 2)
    positions = jnp.arange(D, dtype=jnp.float32) / D
    columns = jnp.arange(KV, dtype=jnp.float32) / KV
    replicas = jnp.arange(REPLICAS, dtype=jnp.float32) / max(REPLICAS - 1, 1)
    row_scale = (3.0 ** positions)[None, None, :, None] * 10.0 ** (spread * jax.random.uniform(key_rows, (1, MATS, D, 1)))
    col_scale = (3.0 ** columns)[None, None, None, :] * 10.0 ** (spread * jax.random.uniform(key_cols, (1, MATS, 1, KV)))
    rep_scale = (3.0 ** replicas)[:, None, None, None]
    return row_scale * col_scale * rep_scale / 10.0


def draw_grad(key, part):
    key = jax.random.fold_in(key, 3)
    scales = scale_field(jax.random.fold_in(key, 11), 0.5)
    values = jnp.clip(jax.random.normal(jax.random.fold_in(key, 12), (REPLICAS, MATS, D, KV)), -4.0, 4.0) * scales
    return values.astype(jnp.bfloat16)


def draw_momentum(key, part):
    key = jax.random.fold_in(key, 5)
    scales = scale_field(jax.random.fold_in(key, 21), 0.5)
    values = jnp.clip(jax.random.normal(jax.random.fold_in(key, 22), (REPLICAS, MATS, D, KV)), -4.0, 4.0) * scales
    return values.astype(jnp.float32)


def shard_levels(rng, dims, cuts, least, top_value):
    def one(dim, blocks):
        heights = jax.random.uniform(jax.random.fold_in(jax.random.fold_in(rng, 6), dim), (blocks,), jnp.float32, least / len(cuts), top_value / len(cuts))
        return jnp.repeat(jnp.exp(heights), dims[dim] // blocks).reshape((-1,) + (1,) * (len(dims) - dim - 1))

    factor_of = one(*cuts[0])
    for cut in cuts[1:]:
        factor_of = factor_of * one(*cut)
    return factor_of


def bell_draw(key, shape, width, bound, shards=(), kind=jnp.bfloat16):
    values = width * jax.random.normal(key, shape, jnp.float32)
    if shards:
        values = values * shard_levels(key, shape, shards, -0.22, 0.18)
    return jnp.clip(values, -bound, bound).astype(kind)


def setup_inputs(seed: int = 0) -> dict:
    splits = jax.random.split(jax.random.key(seed), 4)
    return {
        "grad": draw_grad(jax.random.fold_in(splits[3], 71), 0),
        "momentum": draw_momentum(jax.random.fold_in(splits[3], 71), 0),
        "right_factor": bell_draw(splits[2], (KV, MATS, RANK), KV ** -0.5, 0.1875, ((0, 8),), jnp.float32),
    }


epsilon = 1e-06
decay_keep = 0.1
highest = lax.Precision.HIGHEST

def orthonormal(tall_rows, gram_sum):
    cholesky_factor = jnp.linalg.cholesky(gram_sum)
    identity = jnp.broadcast_to(jnp.eye(gram_sum.shape[-1], dtype=jnp.float32), gram_sum.shape)
    inverse = lax.linalg.triangular_solve(cholesky_factor, identity, left_side=True, lower=True)
    return jnp.einsum('rmk,mlk->rml', tall_rows, inverse, precision=highest)

def reference(grad, momentum, right_factor):
    buffer = momentum + grad.astype(jnp.float32)
    mean_buffer = lax.optimization_barrier(jnp.sum(buffer, axis=0)) / REPLICAS
    factor = right_factor
    left_factor = None
    right_values = None
    for repeat in range(ITERS):
        left_factor = jnp.einsum('mrc,cmk->rmk', mean_buffer, factor, precision=highest)
        gram_sum = jnp.einsum('rmk,rml->mkl', left_factor, left_factor, precision=highest)
        left_factor = orthonormal(left_factor, gram_sum)
        right_values = jnp.einsum('mrc,rmk->cmk', mean_buffer, left_factor, precision=highest)
        squares = lax.optimization_barrier(jnp.sum(right_values * right_values, axis=0))
        factor = right_values / jnp.sqrt(squares + epsilon)
    feedback = jnp.einsum('rmk,cmk->mrc', left_factor, right_values, precision=highest)
    momentum_next = buffer - decay_keep * feedback[None]
    factor_scale = math.sqrt(D * KV / RANK)
    update = (factor_scale * jnp.einsum('rmk,cmk->mrc', left_factor, factor, precision=highest)).astype(jnp.bfloat16)
    return (momentum_next, update, factor)
```

```python
import math

import jax
import jax.numpy as jnp
from jax import lax
from jax.experimental import pallas as pl
from jax.experimental.pallas import tpu as pltpu
from jax.sharding import Mesh, PartitionSpec as P

D = 8192
KV = 1024
RANK = 256
ITERS = 2
NX, NC, NY, NZ = 4, 2, 4, 8
BLOCK = 64

epsilon = 1e-06
decay_keep = 0.1
highest = lax.Precision.HIGHEST


def dot(a, b, contract):
    return lax.dot_general(
        a, b, (contract, ((), ())), precision=highest, preferred_element_type=jnp.float32
    )


def small_inverse_factor(block):
    size = block.shape[0]
    row_ids = lax.broadcasted_iota(jnp.int32, (size, size), 0)
    col_ids = lax.broadcasted_iota(jnp.int32, (size, size), 1)
    work = jnp.concatenate([block, (row_ids == col_ids).astype(jnp.float32)], axis=1)
    ids = lax.broadcasted_iota(jnp.int32, (size, 1), 0)
    pivots = jnp.zeros((size, 1), jnp.float32)
    for j in range(size):
        pivot = work[j : j + 1, j : j + 1]
        pivots = jnp.where(ids == j, pivot, pivots)
        if j < size - 1:
            factors = jnp.where(ids > j, work[:, j : j + 1] * (1.0 / pivot), 0.0)
            work = work - factors * work[j : j + 1, :]
    return work[:, size:] * lax.rsqrt(pivots)


def inverse_factor_kernel(gram_ref, out_ref):
    out_ref[...] = gram_ref[...]
    for lo in range(0, RANK, BLOCK):
        hi = lo + BLOCK
        rows = out_ref[lo:hi, :]
        inverse = small_inverse_factor(rows[:, lo:hi])
        scaled = dot(inverse, rows, ((1,), (0,)))
        parts = [scaled[:, :lo]] if lo else []
        parts.append(inverse)
        if hi < RANK:
            parts.append(scaled[:, hi:])
        pivot_rows = jnp.concatenate(parts, axis=1)
        if hi < RANK:
            update = dot(scaled[:, hi:], pivot_rows, ((0,), (0,)))
            below = out_ref[hi:, :]
            cols = lax.broadcasted_iota(jnp.int32, below.shape, 1)
            out_ref[hi:, :] = jnp.where((cols >= lo) & (cols < hi), 0.0, below) - update
        cols = lax.broadcasted_iota(jnp.int32, pivot_rows.shape, 1)
        out_ref[lo:hi, :] = jnp.where(cols < hi, pivot_rows, 0.0)


def inverse_factor(gram):
    return pl.pallas_call(
        inverse_factor_kernel,
        out_shape=jax.ShapeDtypeStruct((RANK, RANK), jnp.float32),
        name="inverse_factor",
    )(gram)


def ring(size, step):
    return [(k, (k + step) % size) for k in range(size)]


def reduce_scatter_x(pieces):
    here = lax.axis_index("x")
    pick = lambda d: lax.dynamic_index_in_dim(pieces, (here + d) % NX, 0, False)
    came = [lax.ppermute(pick(d), "x", ring(NX, d)) for d in (2, 1, 3)]
    total = pick(0)
    for piece in came:
        total = total + piece
    return total


def gather_columns(block):
    up, down = ring(NZ, 1), ring(NZ, -1)
    below = above = block
    belows, aboves = [], []
    for step in range(NZ // 2):
        below = lax.ppermute(below, "col", up)
        belows.append(below)
        if step < NZ // 2 - 1:
            above = lax.ppermute(above, "col", down)
            aboves.append(above)
    return jnp.concatenate([block] + aboves + belows[::-1], axis=1)


def sum_over_rows(partial):
    share = lax.all_to_all(partial.reshape(NX * NY, -1, RANK), ("x", "row"), 0, 0)
    share = jnp.sum(share, axis=0)
    spread = jnp.broadcast_to(share[None], (NX * NY,) + share.shape)
    return lax.all_to_all(spread, ("x", "row"), 0, 0).reshape(KV, RANK)


def shards(grad, momentum, right_factor):
    core = lax.axis_index("core")
    col = lax.axis_index("col")
    swap = [(0, 1), (1, 0)]

    own_factor = lax.dynamic_index_in_dim(right_factor, core, 1, False)
    factor = lax.all_gather(own_factor, "col", axis=0, tiled=True)
    factor = jnp.roll(factor, -col * (KV // NZ), axis=0)

    buffer = momentum[0] + grad[0].astype(jnp.float32)
    mine = lax.dynamic_index_in_dim(buffer, core, 0, False)
    other = lax.dynamic_index_in_dim(buffer, 1 - core, 0, False)
    mine = mine + lax.ppermute(other, "core", swap)
    block = reduce_scatter_x(mine.reshape(NX, -1, mine.shape[-1])) / (NX * NC)
    rows = gather_columns(block)

    for repeat in range(ITERS):
        left = dot(rows, factor, ((1,), (0,)))
        if repeat == ITERS - 1:
            lefts = lax.all_gather(left, ("x", "core"), axis=0)
        product = sum_over_rows(dot(rows, left, ((0,), (0,))))
        inverse = inverse_factor(dot(factor, product, ((0,), (0,))))
        right = dot(product, inverse, ((1,), (1,)))
        squares = jnp.sum(right * right, axis=0)
        factor = right / jnp.sqrt(squares + epsilon)

    width = KV // NZ
    factor_scale = math.sqrt(D * KV / RANK)
    own_next = factor[:width]
    stacked = jnp.concatenate([right[:width], own_next], axis=0)
    folded = dot(stacked, inverse, ((1,), (0,)))
    sent = jnp.concatenate([folded, own_next], axis=0)
    got = lax.ppermute(sent, "core", swap)
    pair = jnp.where(core == 0, jnp.stack([sent, got]), jnp.stack([got, sent]))

    lefts = lefts.reshape(NX, NC, -1, RANK)
    outs = jnp.einsum("xmrk,mck->mxrc", lefts, pair[:, : 2 * width], precision=highest)
    outs = outs.reshape(NC, -1, 2 * width)
    momentum_next = buffer - decay_keep * outs[:, :, :width]
    update = (factor_scale * outs[:, :, width:]).astype(jnp.bfloat16)
    factor_next = jnp.stack([pair[0, 2 * width :], pair[1, 2 * width :]], axis=1)
    return momentum_next[None], update, factor_next


def solution(mesh):
    split = Mesh(mesh.devices.reshape(NX, NC, NY, NZ), ("x", "core", "row", "col"))
    data = P(("x", "core"), None, "row", "col")
    return jax.shard_map(
        shards,
        mesh=split,
        in_specs=(data, data, P("col", None, None)),
        out_specs=(data, P(None, "row", "col"), P("col", None, None)),
        check_vma=False,
    )
```

```python
import math

import jax
import jax.numpy as jnp
from jax import lax
from jax.experimental import pallas as pl
from jax.experimental.pallas import tpu as pltpu
from jax.sharding import Mesh, PartitionSpec as P

D = 8192
KV = 1024
RANK = 256
ITERS = 2
NX, NC, NY, NZ = 4, 2, 4, 8
BLOCK = 64
QUAD = 4
WIDTH = KV // NZ

epsilon = 1e-06
decay_keep = 0.1
highest = lax.Precision.HIGHEST


def dot(a, b, contract):
    return lax.dot_general(
        a, b, (contract, ((), ())), precision=highest, preferred_element_type=jnp.float32
    )


def small_inverse_factor(block):
    size = block.shape[0]
    count = size // 8
    chunks = [block[8 * c : 8 * c + 8] for c in range(count)]
    sub = lax.broadcasted_iota(jnp.int32, (8, size), 0)
    lane = lax.broadcasted_iota(jnp.int32, (8, size), 1)
    pivots = []
    for p in range(count):
        lo = 8 * p
        spread = {}
        for c in range(p, count):
            for k in range(8):
                spread[k, c] = jnp.broadcast_to(chunks[c][:, lo + k : lo + k + 1], (8, size))
        panel = (lane >= lo) & (lane < lo + 8)
        for c in range(p, count):
            unit = jnp.where(lane == sub + lo, 1.0, 0.0) if c == p else 0.0
            chunks[c] = jnp.where(panel, unit, chunks[c])
        held = None
        for j in range(8):
            pivot = jnp.broadcast_to(spread[j, p][j : j + 1, :], (8, size))
            held = pivot if held is None else jnp.where(sub >= j, pivot, held)
            scale = pltpu.reciprocal(pivot, approx=True)
            row = jnp.broadcast_to(chunks[p][j : j + 1, :], (8, size)) * scale
            heads = {
                k: jnp.broadcast_to(spread[k, p][j : j + 1, :], (8, size)) * scale
                for k in range(j + 1, 8)
            }
            for c in range(p, count):
                column = spread[j, c]
                if c == p:
                    column = jnp.where(sub > j, column, 0.0)
                chunks[c] = chunks[c] - column * row
                for k in heads:
                    spread[k, c] = spread[k, c] - column * heads[k]
        pivots.append(held)
    inverse = jnp.concatenate([c * lax.rsqrt(d) for c, d in zip(chunks, pivots)], axis=0)
    row_ids = lax.broadcasted_iota(jnp.int32, (size, size), 0)
    col_ids = lax.broadcasted_iota(jnp.int32, (size, size), 1)
    return jnp.where(col_ids <= row_ids, inverse, 0.0)


def inverse_factor(gram, out_ref):
    out_ref[...] = gram
    for lo in range(0, RANK, BLOCK):
        hi = lo + BLOCK
        rows = out_ref[lo:hi, :]
        inverse = small_inverse_factor(rows[:, lo:hi])
        scaled = dot(inverse, rows, ((1,), (0,)))
        parts = [scaled[:, :lo]] if lo else []
        parts.append(inverse)
        if hi < RANK:
            parts.append(scaled[:, hi:])
        pivot_rows = jnp.concatenate(parts, axis=1)
        if hi < RANK:
            update = dot(scaled[:, hi:], pivot_rows, ((0,), (0,)))
            below = out_ref[hi:, :]
            cols = lax.broadcasted_iota(jnp.int32, below.shape, 1)
            out_ref[hi:, :] = jnp.where((cols >= lo) & (cols < hi), 0.0, below) - update
        cols = lax.broadcasted_iota(jnp.int32, pivot_rows.shape, 1)
        out_ref[lo:hi, :] = jnp.where(cols < hi, pivot_rows, 0.0)


def orthonormal_right(product_ref, factor_ref, inverse_ref, right_ref):
    step = 2 * RANK
    chunk = lambda ref, c: ref[pl.ds(pl.multiple_of(c * step, step), step), :]
    zero = jnp.zeros((RANK, RANK), jnp.float32)
    add = lambda c, gram: gram + dot(chunk(factor_ref, c), chunk(product_ref, c), ((0,), (0,)))
    inverse_factor(lax.fori_loop(0, KV // step, add, zero), inverse_ref)

    def scale(c, squares):
        right = dot(chunk(product_ref, c), inverse_ref[...], ((1,), (1,)))
        right_ref[pl.ds(pl.multiple_of(c * step, step), step), :] = right
        return squares + jnp.sum(right * right, axis=0, keepdims=True)

    squares = lax.fori_loop(0, KV // step, scale, jnp.zeros((1, RANK), jnp.float32))
    return jnp.sqrt(squares + epsilon)


def next_factor_kernel(product_ref, factor_ref, out_ref, inverse_ref):
    norms = orthonormal_right(product_ref, factor_ref, inverse_ref, out_ref)
    out_ref[...] = out_ref[...] / norms


def last_factor_kernel(col_ref, product_ref, factor_ref, out_ref, inverse_ref, right_ref):
    norms = orthonormal_right(product_ref, factor_ref, inverse_ref, right_ref)
    right = right_ref[pl.ds(pl.multiple_of(col_ref[0] * WIDTH, WIDTH), WIDTH), :]
    factor = right / norms
    scale = math.sqrt(D * KV / RANK)
    stacked = jnp.concatenate([decay_keep * right, scale * factor], axis=0)
    out_ref[:RANK, :] = dot(stacked, inverse_ref[...], ((1,), (0,))).T
    out_ref[RANK:, :] = factor


vmem = pltpu.CompilerParams(vmem_limit_bytes=32 * 2**20)


def next_factor(product, factor):
    return pl.pallas_call(
        next_factor_kernel,
        out_shape=jax.ShapeDtypeStruct((KV, RANK), jnp.float32),
        scratch_shapes=[pltpu.VMEM((RANK, RANK), jnp.float32)],
        compiler_params=vmem,
        name="next_factor",
    )(product, factor)


def last_factor(col, product, factor):
    whole = pl.BlockSpec(memory_space=pltpu.VMEM)
    return pl.pallas_call(
        last_factor_kernel,
        in_specs=[pl.BlockSpec(memory_space=pltpu.SMEM), whole, whole],
        out_shape=jax.ShapeDtypeStruct((RANK + WIDTH, RANK), jnp.float32),
        scratch_shapes=[
            pltpu.VMEM((RANK, RANK), jnp.float32),
            pltpu.VMEM((KV, RANK), jnp.float32),
        ],
        compiler_params=vmem,
        name="last_factor",
    )(col[None], product, factor)


def halves(value):
    high = value.astype(jnp.bfloat16)
    return high, (value - high.astype(jnp.float32)).astype(jnp.bfloat16)


def output_kernel(
    core_ref, left_ref, own_ref, got_ref, momentum_ref, grad_ref,
    momentum_out, update_out, factor_out,
):
    matrix = pl.program_id(0)
    weight = jnp.where(matrix == core_ref[0], own_ref[:RANK, :], got_ref[:RANK, :])
    high, low = halves(weight)
    product = lambda a, b: jnp.dot(a, b, preferred_element_type=jnp.float32)
    rows = left_ref.shape[2]
    for x in range(NX):
        left_high, left_low = halves(left_ref[x, 0])
        both = product(left_low, high) + product(left_high, low) + product(left_high, high)
        here = slice(x * rows, (x + 1) * rows)
        buffer = momentum_ref[0, 0, here] + grad_ref[0, 0, here].astype(jnp.float32)
        momentum_out[0, 0, here] = buffer - both[:, :WIDTH]
        update_out[0, here] = both[:, WIDTH:].astype(jnp.bfloat16)

    @pl.when(matrix == 0)
    def _():
        first = core_ref[0] == 0
        mine, other = own_ref[RANK:, :], got_ref[RANK:, :]
        factor_out[:, 0, :] = jnp.where(first, mine, other)
        factor_out[:, 1, :] = jnp.where(first, other, mine)


def outputs(core, lefts, own, got, momentum, grad):
    rows = momentum.shape[2]
    data = pl.BlockSpec((1, 1, rows, WIDTH), lambda m: (0, m, 0, 0))
    weight = pl.BlockSpec((RANK + WIDTH, RANK), lambda m: (0, 0))
    return pl.pallas_call(
        output_kernel,
        grid=(NC,),
        in_specs=[
            pl.BlockSpec(memory_space=pltpu.SMEM),
            pl.BlockSpec((NX, 1, rows // NX, RANK), lambda m: (0, m, 0, 0)),
            weight,
            weight,
            data,
            data,
        ],
        out_specs=[
            data,
            pl.BlockSpec((1, rows, WIDTH), lambda m: (m, 0, 0)),
            pl.BlockSpec((WIDTH, NC, RANK), lambda m: (0, 0, 0)),
        ],
        out_shape=[
            jax.ShapeDtypeStruct(momentum.shape, jnp.float32),
            jax.ShapeDtypeStruct(momentum.shape[1:], jnp.bfloat16),
            jax.ShapeDtypeStruct((WIDTH, NC, RANK), jnp.float32),
        ],
        compiler_params=pltpu.CompilerParams(vmem_limit_bytes=56 * 2**20),
        name="outputs",
    )(core[None], lefts.reshape(NX, NC, -1, RANK), own, got, momentum, grad)


def ring(size, step):
    return [(k, (k + step) % size) for k in range(size)]


def share_quad(share):
    place = lax.rem(lax.axis_index("col"), QUAD)
    whole = jnp.zeros((QUAD,) + share.shape, share.dtype)
    parts = [(0, share)]
    for d in range(1, QUAD):
        pairs = [(k, k // QUAD * QUAD + (k + d) % QUAD) for k in range(NZ)]
        parts.append((QUAD - d, lax.ppermute(share, "col", pairs)))
    for offset, part in parts:
        whole = lax.dynamic_update_index_in_dim(whole, part, lax.rem(place + offset, QUAD), 0)
    return whole


def sum_over_rows(rows, left):
    place = lax.rem(lax.axis_index("col"), QUAD)
    part = KV // QUAD
    columns = lax.dynamic_slice_in_dim(rows, place * part, part, 1)
    partial = dot(columns, left, ((0,), (0,)))
    share = lax.all_to_all(partial.reshape(NX * NY, -1, RANK), ("x", "row"), 0, 0)
    share = share_quad(jnp.sum(share, axis=0))
    spread = jnp.broadcast_to(share[None], (NX * NY,) + share.shape)
    whole = lax.all_to_all(spread, ("x", "row"), 0, 0)
    return jnp.swapaxes(whole, 0, 1).reshape(KV, RANK)


def gather_rows(grad, momentum):
    core, x, z = (lax.axis_index(name) for name in ("core", "x", "col"))
    pick = lambda array, m: lax.dynamic_index_in_dim(array[0], m, 0, False)
    buffer = lambda m: pick(momentum, m) + pick(grad, m).astype(jnp.float32)

    came = lax.ppermute(buffer(1 - core), "core", [(0, 1), (1, 0)])
    pieces = (buffer(core) + came).reshape(NX, -1, WIDTH)
    piece = lambda d: lax.dynamic_index_in_dim(pieces, lax.rem(x + d, NX), 0, False)
    came = [lax.ppermute(piece(d), "x", ring(NX, d)) for d in (2, 1, 3)]
    block = (piece(0) + came[1] + came[2] + came[0]) / (NX * NC)

    up, down = ring(NZ, 1), ring(NZ, -1)
    below = above = block
    parts = [(0, block)]
    for step in range(1, NZ // 2 + 1):
        below = lax.ppermute(below, "col", up)
        parts.append((NZ - step, below))
        if step < NZ // 2:
            above = lax.ppermute(above, "col", down)
            parts.append((step, above))
    rows = jnp.zeros((block.shape[0], KV), jnp.float32)
    for offset, part in parts:
        rows = lax.dynamic_update_slice(rows, part, (0, lax.rem(z + offset, NZ) * WIDTH))
    return rows


def shards(grad, momentum, right_factor):
    core = lax.axis_index("core")
    own_factor = lax.dynamic_index_in_dim(right_factor, core, 1, False)
    factor = lax.all_gather(own_factor, "col", axis=0, tiled=True)
    rows = gather_rows(grad, momentum)

    for repeat in range(ITERS):
        left = dot(rows, factor, ((1,), (0,)))
        product = sum_over_rows(rows, left)
        if repeat < ITERS - 1:
            factor = next_factor(product, factor)
    lefts = lax.all_gather(left, ("x", "core"), axis=0)

    sent = last_factor(lax.axis_index("col"), product, factor)
    got = lax.ppermute(sent, "core", [(0, 1), (1, 0)])
    return tuple(outputs(core, lefts, sent, got, momentum, grad))


def solution(mesh):
    split = Mesh(mesh.devices.reshape(NX, NC, NY, NZ), ("x", "core", "row", "col"))
    data = P(("x", "core"), None, "row", "col")
    return jax.shard_map(
        shards,
        mesh=split,
        in_specs=(data, data, P("col", None, None)),
        out_specs=(data, P(None, "row", "col"), P("col", None, None)),
        check_vma=False,
    )
```

```python
import math

import jax
import jax.numpy as jnp
from jax import lax
from jax.experimental import pallas as pl
from jax.experimental.pallas import tpu as pltpu
from jax.sharding import Mesh, PartitionSpec as P

D = 8192
KV = 1024
RANK = 256
ITERS = 2
NX, NC, NY, NZ = 4, 2, 4, 8
COL = ("quad", "place")
BLOCK = 64
PANEL = 16
QUAD = 4
WIDTH = KV // NZ

epsilon = 1e-06
decay_keep = 0.1
highest = lax.Precision.HIGHEST


def dot(a, b, contract):
    return lax.dot_general(
        a, b, (contract, ((), ())), precision=highest, preferred_element_type=jnp.float32
    )


def small_inverse_factor(block):
    size = block.shape[0]
    count = size // 8
    chunks = [block[8 * c : 8 * c + 8] for c in range(count)]
    sub = lax.broadcasted_iota(jnp.int32, (8, size), 0)
    lane = lax.broadcasted_iota(jnp.int32, (8, size), 1)
    pivots = [None] * count
    for lo in range(0, size, PANEL):
        spread = {}
        for c in range(lo // 8, count):
            for k in range(PANEL):
                spread[k, c] = jnp.broadcast_to(chunks[c][:, lo + k : lo + k + 1], (8, size))
        panel = (lane >= lo) & (lane < lo + PANEL)
        for c in range(lo // 8, count):
            unit = jnp.where(lane == sub + 8 * c, 1.0, 0.0) if 8 * c < lo + PANEL else 0.0
            chunks[c] = jnp.where(panel, unit, chunks[c])
        for j in range(PANEL):
            p, row = divmod(lo + j, 8)
            pivot = jnp.broadcast_to(spread[j, p][row : row + 1, :], (8, size))
            pivots[p] = jnp.where(sub >= row, pivot, pivot if row == 0 else pivots[p])
            scale = pltpu.reciprocal(pivot, approx=True)
            head = jnp.broadcast_to(chunks[p][row : row + 1, :], (8, size)) * scale
            heads = {
                k: jnp.broadcast_to(spread[k, p][row : row + 1, :], (8, size)) * scale
                for k in range(j + 1, PANEL)
            }
            for c in range(p, count):
                column = spread[j, c]
                if c == p:
                    column = jnp.where(sub > row, column, 0.0)
                chunks[c] = chunks[c] - column * head
                for k in heads:
                    spread[k, c] = spread[k, c] - column * heads[k]
    inverse = jnp.concatenate([c * lax.rsqrt(d) for c, d in zip(chunks, pivots)], axis=0)
    row_ids = lax.broadcasted_iota(jnp.int32, (size, size), 0)
    col_ids = lax.broadcasted_iota(jnp.int32, (size, size), 1)
    return jnp.where(col_ids <= row_ids, inverse, 0.0)


def inverse_factor(gram, out_ref):
    out_ref[...] = gram
    for lo in range(0, RANK, BLOCK):
        hi = lo + BLOCK
        rows = out_ref[lo:hi, :]
        inverse = small_inverse_factor(rows[:, lo:hi])
        scaled = dot(inverse, rows, ((1,), (0,)))
        parts = [scaled[:, :lo]] if lo else []
        parts.append(inverse)
        if hi < RANK:
            parts.append(scaled[:, hi:])
        pivot_rows = jnp.concatenate(parts, axis=1)
        if hi < RANK:
            update = dot(scaled[:, hi:], pivot_rows, ((0,), (0,)))
            below = out_ref[hi:, :]
            cols = lax.broadcasted_iota(jnp.int32, below.shape, 1)
            out_ref[hi:, :] = jnp.where((cols >= lo) & (cols < hi), 0.0, below) - update
        cols = lax.broadcasted_iota(jnp.int32, pivot_rows.shape, 1)
        out_ref[lo:hi, :] = jnp.where(cols < hi, pivot_rows, 0.0)


def orthonormal_right(product_ref, factor_ref, inverse_ref, right_ref):
    step = 2 * RANK
    chunk = lambda ref, c: ref[pl.ds(pl.multiple_of(c * step, step), step), :]
    zero = jnp.zeros((RANK, RANK), jnp.float32)
    add = lambda c, gram: gram + dot(chunk(factor_ref, c), chunk(product_ref, c), ((0,), (0,)))
    inverse_factor(lax.fori_loop(0, KV // step, add, zero), inverse_ref)

    def scale(c, squares):
        right = dot(chunk(product_ref, c), inverse_ref[...], ((1,), (1,)))
        right_ref[pl.ds(pl.multiple_of(c * step, step), step), :] = right
        return squares + jnp.sum(right * right, axis=0, keepdims=True)

    squares = lax.fori_loop(0, KV // step, scale, jnp.zeros((1, RANK), jnp.float32))
    return jnp.sqrt(squares + epsilon)


def next_factor_kernel(product_ref, factor_ref, out_ref, inverse_ref):
    norms = orthonormal_right(product_ref, factor_ref, inverse_ref, out_ref)
    out_ref[...] = out_ref[...] / norms


def last_factor_kernel(col_ref, product_ref, factor_ref, out_ref, inverse_ref, right_ref):
    norms = orthonormal_right(product_ref, factor_ref, inverse_ref, right_ref)
    right = right_ref[pl.ds(pl.multiple_of(col_ref[0] * WIDTH, WIDTH), WIDTH), :]
    factor = right / norms
    scale = math.sqrt(D * KV / RANK)
    stacked = jnp.concatenate([decay_keep * right, scale * factor], axis=0)
    out_ref[:RANK, :] = dot(stacked, inverse_ref[...], ((1,), (0,))).T
    out_ref[RANK:, :] = factor


vmem = pltpu.CompilerParams(vmem_limit_bytes=32 * 2**20)


def next_factor(product, factor):
    return pl.pallas_call(
        next_factor_kernel,
        out_shape=jax.ShapeDtypeStruct((KV, RANK), jnp.float32),
        scratch_shapes=[pltpu.VMEM((RANK, RANK), jnp.float32)],
        compiler_params=vmem,
        name="next_factor",
    )(product, factor)


def last_factor(col, product, factor):
    whole = pl.BlockSpec(memory_space=pltpu.VMEM)
    return pl.pallas_call(
        last_factor_kernel,
        in_specs=[pl.BlockSpec(memory_space=pltpu.SMEM), whole, whole],
        out_shape=jax.ShapeDtypeStruct((RANK + WIDTH, RANK), jnp.float32),
        scratch_shapes=[
            pltpu.VMEM((RANK, RANK), jnp.float32),
            pltpu.VMEM((KV, RANK), jnp.float32),
        ],
        compiler_params=vmem,
        name="last_factor",
    )(col[None], product, factor)


def halves(value):
    high = value.astype(jnp.bfloat16)
    return high, (value - high.astype(jnp.float32)).astype(jnp.bfloat16)


def output_kernel(
    core_ref, left_ref, own_ref, got_ref, momentum_ref, grad_ref,
    momentum_out, update_out, factor_out,
):
    matrix = pl.program_id(0)
    weight = jnp.where(matrix == core_ref[0], own_ref[:RANK, :], got_ref[:RANK, :])
    high, low = halves(weight)
    product = lambda a, b: jnp.dot(a, b, preferred_element_type=jnp.float32)
    rows = left_ref.shape[2]
    for x in range(NX):
        left_high, left_low = halves(left_ref[x, 0])
        both = product(left_low, high) + product(left_high, low) + product(left_high, high)
        here = slice(x * rows, (x + 1) * rows)
        buffer = momentum_ref[0, 0, here] + grad_ref[0, 0, here].astype(jnp.float32)
        momentum_out[0, 0, here] = buffer - both[:, :WIDTH]
        update_out[0, here] = both[:, WIDTH:].astype(jnp.bfloat16)

    @pl.when(matrix == 0)
    def _():
        first = core_ref[0] == 0
        mine, other = own_ref[RANK:, :], got_ref[RANK:, :]
        factor_out[:, 0, :] = jnp.where(first, mine, other)
        factor_out[:, 1, :] = jnp.where(first, other, mine)


def outputs(core, lefts, own, got, momentum, grad):
    rows = momentum.shape[2]
    data = pl.BlockSpec((1, 1, rows, WIDTH), lambda m: (0, m, 0, 0))
    weight = pl.BlockSpec((RANK + WIDTH, RANK), lambda m: (0, 0))
    return pl.pallas_call(
        output_kernel,
        grid=(NC,),
        in_specs=[
            pl.BlockSpec(memory_space=pltpu.SMEM),
            pl.BlockSpec((NX, 1, rows // NX, RANK), lambda m: (0, m, 0, 0)),
            weight,
            weight,
            data,
            data,
        ],
        out_specs=[
            data,
            pl.BlockSpec((1, rows, WIDTH), lambda m: (m, 0, 0)),
            pl.BlockSpec((WIDTH, NC, RANK), lambda m: (0, 0, 0)),
        ],
        out_shape=[
            jax.ShapeDtypeStruct(momentum.shape, jnp.float32),
            jax.ShapeDtypeStruct(momentum.shape[1:], jnp.bfloat16),
            jax.ShapeDtypeStruct((WIDTH, NC, RANK), jnp.float32),
        ],
        compiler_params=pltpu.CompilerParams(vmem_limit_bytes=56 * 2**20),
        name="outputs",
    )(core[None], lefts.reshape(NX, NC, -1, RANK), own, got, momentum, grad)


def ring(size, step):
    return [(k, (k + step) % size) for k in range(size)]


def share_quad(share):
    place = lax.rem(lax.axis_index(COL), QUAD)
    whole = jnp.zeros((QUAD,) + share.shape, share.dtype)
    parts = [(0, share)]
    for d in range(1, QUAD):
        pairs = [(k, k // QUAD * QUAD + (k + d) % QUAD) for k in range(NZ)]
        parts.append((QUAD - d, lax.ppermute(share, COL, pairs)))
    for offset, part in parts:
        whole = lax.dynamic_update_index_in_dim(whole, part, lax.rem(place + offset, QUAD), 0)
    return whole


def spread(share, axes, size):
    return lax.all_to_all(jnp.broadcast_to(share[None], (size,) + share.shape), axes, 0, 0)


def sum_over_rows(rows, left, by_row):
    place = lax.rem(lax.axis_index(COL), QUAD)
    part = KV // QUAD
    columns = lax.dynamic_slice_in_dim(rows, place * part, part, 1)
    partial = dot(columns, left, ((0,), (0,)))
    share = lax.all_to_all(partial.reshape(NX * NY, -1, RANK), ("x", "row"), 0, 0)
    share = jnp.sum(share, axis=0)
    if not by_row:
        share = share_quad(share)
        whole = spread(share, ("x", "row"), NX * NY)
        return jnp.swapaxes(whole, 0, 1).reshape(KV, RANK)
    share = spread(share, ("x", "place"), NX * QUAD)
    whole = spread(share, "row", NY).reshape(NY, NX, QUAD, -1, RANK)
    return whole.transpose(2, 1, 0, 3, 4).reshape(KV, RANK)


def gather_rows(grad, momentum):
    core, x, z = (lax.axis_index(name) for name in ("core", "x", COL))
    pick = lambda array, m: lax.dynamic_index_in_dim(array[0], m, 0, False)
    buffer = lambda m: pick(momentum, m) + pick(grad, m).astype(jnp.float32)

    came = lax.ppermute(buffer(1 - core), "core", [(0, 1), (1, 0)])
    pieces = (buffer(core) + came).reshape(NX, -1, WIDTH)
    piece = lambda d: lax.dynamic_index_in_dim(pieces, lax.rem(x + d, NX), 0, False)
    came = [lax.ppermute(piece(d), "x", ring(NX, d)) for d in (2, 1, 3)]
    block = (piece(0) + came[1] + came[2] + came[0]) / (NX * NC)

    up, down = ring(NZ, 1), ring(NZ, -1)
    below = above = block
    parts = [(0, block)]
    for step in range(1, NZ // 2 + 1):
        below = lax.ppermute(below, COL, up)
        parts.append((NZ - step, below))
        if step < NZ // 2:
            above = lax.ppermute(above, COL, down)
            parts.append((step, above))
    rows = jnp.zeros((block.shape[0], KV), jnp.float32)
    for offset, part in parts:
        rows = lax.dynamic_update_slice(rows, part, (0, lax.rem(z + offset, NZ) * WIDTH))
    return rows


def shards(grad, momentum, right_factor):
    core = lax.axis_index("core")
    own_factor = lax.dynamic_index_in_dim(right_factor, core, 1, False)
    factor = lax.all_gather(own_factor, COL, axis=0, tiled=True)
    rows = gather_rows(grad, momentum)

    for repeat in range(ITERS):
        left = dot(rows, factor, ((1,), (0,)))
        product = sum_over_rows(rows, left, by_row=repeat == ITERS - 1)
        if repeat < ITERS - 1:
            factor = next_factor(product, factor)
    lefts = lax.all_gather(left, ("x", "core"), axis=0)

    sent = last_factor(lax.axis_index(COL), product, factor)
    got = lax.ppermute(sent, "core", [(0, 1), (1, 0)])
    return tuple(outputs(core, lefts, sent, got, momentum, grad))


def solution(mesh):
    shape = (NX, NC, NY, NZ // QUAD, QUAD)
    split = Mesh(mesh.devices.reshape(shape), ("x", "core", "row") + COL)
    data = P(("x", "core"), None, "row", COL)
    return jax.shard_map(
        shards,
        mesh=split,
        in_specs=(data, data, P(COL, None, None)),
        out_specs=(data, P(None, "row", COL), P(COL, None, None)),
        check_vma=False,
    )
```

```python
import math

import jax
import jax.numpy as jnp
from jax import lax
from jax.experimental import pallas as pl
from jax.experimental.pallas import tpu as pltpu
from jax.sharding import Mesh, PartitionSpec as P

D = 8192
KV = 1024
RANK = 256
ITERS = 2
NX, NC, NY, NZ = 4, 2, 4, 8
COL = ("quad", "place")
BLOCK = 64
PANEL = 16
QUAD = 4
WIDTH = KV // NZ

epsilon = 1e-06
decay_keep = 0.1
highest = lax.Precision.HIGHEST


def dot(a, b, contract):
    return lax.dot_general(
        a, b, (contract, ((), ())), precision=highest, preferred_element_type=jnp.float32
    )


def small_inverse_factor(block):
    size = block.shape[0]
    count = size // 8
    chunks = [block[8 * c : 8 * c + 8] for c in range(count)]
    sub = lax.broadcasted_iota(jnp.int32, (8, size), 0)
    lane = lax.broadcasted_iota(jnp.int32, (8, size), 1)
    pivots = [None] * count
    for lo in range(0, size, PANEL):
        spread = {}
        for c in range(lo // 8, count):
            for k in range(PANEL):
                spread[k, c] = jnp.broadcast_to(chunks[c][:, lo + k : lo + k + 1], (8, size))
        panel = (lane >= lo) & (lane < lo + PANEL)
        for c in range(lo // 8, count):
            unit = jnp.where(lane == sub + 8 * c, 1.0, 0.0) if 8 * c < lo + PANEL else 0.0
            chunks[c] = jnp.where(panel, unit, chunks[c])
        for j in range(PANEL):
            p, row = divmod(lo + j, 8)
            pivot = jnp.broadcast_to(spread[j, p][row : row + 1, :], (8, size))
            pivots[p] = jnp.where(sub >= row, pivot, pivot if row == 0 else pivots[p])
            scale = pltpu.reciprocal(pivot, approx=True)
            head = jnp.broadcast_to(chunks[p][row : row + 1, :], (8, size)) * scale
            heads = {
                k: jnp.broadcast_to(spread[k, p][row : row + 1, :], (8, size)) * scale
                for k in range(j + 1, PANEL)
            }
            for c in range(p, count):
                column = spread[j, c]
                if c == p:
                    column = jnp.where(sub > row, column, 0.0)
                chunks[c] = chunks[c] - column * head
                for k in heads:
                    spread[k, c] = spread[k, c] - column * heads[k]
    inverse = jnp.concatenate([c * lax.rsqrt(d) for c, d in zip(chunks, pivots)], axis=0)
    row_ids = lax.broadcasted_iota(jnp.int32, (size, size), 0)
    col_ids = lax.broadcasted_iota(jnp.int32, (size, size), 1)
    return jnp.where(col_ids <= row_ids, inverse, 0.0)


def inverse_factor(gram, out_ref):
    out_ref[...] = gram
    for lo in range(0, RANK, BLOCK):
        hi = lo + BLOCK
        rows = out_ref[lo:hi, :]
        inverse = small_inverse_factor(rows[:, lo:hi])
        scaled = dot(inverse, rows, ((1,), (0,)))
        parts = [scaled[:, :lo]] if lo else []
        parts.append(inverse)
        if hi < RANK:
            parts.append(scaled[:, hi:])
        pivot_rows = jnp.concatenate(parts, axis=1)
        if hi < RANK:
            update = dot(scaled[:, hi:], pivot_rows, ((0,), (0,)))
            below = out_ref[hi:, :]
            cols = lax.broadcasted_iota(jnp.int32, below.shape, 1)
            out_ref[hi:, :] = jnp.where((cols >= lo) & (cols < hi), 0.0, below) - update
        cols = lax.broadcasted_iota(jnp.int32, pivot_rows.shape, 1)
        out_ref[lo:hi, :] = jnp.where(cols < hi, pivot_rows, 0.0)


def orthonormal_right(product_ref, factor_ref, inverse_ref, right_ref):
    step = 2 * RANK
    chunk = lambda ref, c: ref[pl.ds(pl.multiple_of(c * step, step), step), :]
    zero = jnp.zeros((RANK, RANK), jnp.float32)
    add = lambda c, gram: gram + dot(chunk(factor_ref, c), chunk(product_ref, c), ((0,), (0,)))
    inverse_factor(lax.fori_loop(0, KV // step, add, zero), inverse_ref)

    def scale(c, squares):
        right = dot(chunk(product_ref, c), inverse_ref[...], ((1,), (1,)))
        right_ref[pl.ds(pl.multiple_of(c * step, step), step), :] = right
        return squares + jnp.sum(right * right, axis=0, keepdims=True)

    squares = lax.fori_loop(0, KV // step, scale, jnp.zeros((1, RANK), jnp.float32))
    return jnp.sqrt(squares + epsilon)


def next_factor_kernel(product_ref, factor_ref, out_ref, inverse_ref):
    norms = orthonormal_right(product_ref, factor_ref, inverse_ref, out_ref)
    out_ref[...] = out_ref[...] / norms


def last_factor_kernel(col_ref, product_ref, factor_ref, out_ref, inverse_ref, right_ref):
    norms = orthonormal_right(product_ref, factor_ref, inverse_ref, right_ref)
    right = right_ref[pl.ds(pl.multiple_of(col_ref[0] * WIDTH, WIDTH), WIDTH), :]
    factor = right / norms
    scale = math.sqrt(D * KV / RANK)
    stacked = jnp.concatenate([decay_keep * right, scale * factor], axis=0)
    out_ref[:RANK, :] = dot(stacked, inverse_ref[...], ((1,), (0,))).T
    out_ref[RANK:, :] = factor


vmem = pltpu.CompilerParams(vmem_limit_bytes=32 * 2**20)


def next_factor(product, factor):
    return pl.pallas_call(
        next_factor_kernel,
        out_shape=jax.ShapeDtypeStruct((KV, RANK), jnp.float32),
        scratch_shapes=[pltpu.VMEM((RANK, RANK), jnp.float32)],
        compiler_params=vmem,
        name="next_factor",
    )(product, factor)


def last_factor(col, product, factor):
    whole = pl.BlockSpec(memory_space=pltpu.VMEM)
    return pl.pallas_call(
        last_factor_kernel,
        in_specs=[pl.BlockSpec(memory_space=pltpu.SMEM), whole, whole],
        out_shape=jax.ShapeDtypeStruct((RANK + WIDTH, RANK), jnp.float32),
        scratch_shapes=[
            pltpu.VMEM((RANK, RANK), jnp.float32),
            pltpu.VMEM((KV, RANK), jnp.float32),
        ],
        compiler_params=vmem,
        name="last_factor",
    )(col[None], product, factor)


def halves(value):
    high = value.astype(jnp.bfloat16)
    return high, (value - high.astype(jnp.float32)).astype(jnp.bfloat16)


def output_kernel(
    core_ref, left_ref, own_ref, got_ref, momentum_ref, grad_ref,
    momentum_out, update_out, factor_out,
):
    matrix = pl.program_id(0)
    weight = jnp.where(matrix == core_ref[0], own_ref[:RANK, :], got_ref[:RANK, :])
    high, low = halves(weight)
    product = lambda a, b: jnp.dot(a, b, preferred_element_type=jnp.float32)
    rows = left_ref.shape[2]
    for x in range(NX):
        left_high, left_low = halves(left_ref[x, 0])
        both = product(left_low, high) + product(left_high, low) + product(left_high, high)
        here = slice(x * rows, (x + 1) * rows)
        buffer = momentum_ref[0, 0, here] + grad_ref[0, 0, here].astype(jnp.float32)
        momentum_out[0, 0, here] = buffer - both[:, :WIDTH]
        update_out[0, here] = both[:, WIDTH:].astype(jnp.bfloat16)

    @pl.when(matrix == 0)
    def _():
        first = core_ref[0] == 0
        mine, other = own_ref[RANK:, :], got_ref[RANK:, :]
        factor_out[:, 0, :] = jnp.where(first, mine, other)
        factor_out[:, 1, :] = jnp.where(first, other, mine)


def outputs(core, lefts, own, got, momentum, grad):
    rows = momentum.shape[2]
    data = pl.BlockSpec((1, 1, rows, WIDTH), lambda m: (0, m, 0, 0))
    weight = pl.BlockSpec((RANK + WIDTH, RANK), lambda m: (0, 0))
    return pl.pallas_call(
        output_kernel,
        grid=(NC,),
        in_specs=[
            pl.BlockSpec(memory_space=pltpu.SMEM),
            pl.BlockSpec((NX, 1, rows // NX, RANK), lambda m: (0, m, 0, 0)),
            weight,
            weight,
            data,
            data,
        ],
        out_specs=[
            data,
            pl.BlockSpec((1, rows, WIDTH), lambda m: (m, 0, 0)),
            pl.BlockSpec((WIDTH, NC, RANK), lambda m: (0, 0, 0)),
        ],
        out_shape=[
            jax.ShapeDtypeStruct(momentum.shape, jnp.float32),
            jax.ShapeDtypeStruct(momentum.shape[1:], jnp.bfloat16),
            jax.ShapeDtypeStruct((WIDTH, NC, RANK), jnp.float32),
        ],
        compiler_params=pltpu.CompilerParams(vmem_limit_bytes=56 * 2**20),
        name="outputs",
    )(core[None], lefts.reshape(NX, NC, -1, RANK), own, got, momentum, grad)


def ring(size, step):
    return [(k, (k + step) % size) for k in range(size)]


def share_quad(share):
    place = lax.rem(lax.axis_index(COL), QUAD)
    whole = jnp.zeros((QUAD,) + share.shape, share.dtype)
    parts = [(0, share)]
    for d in range(1, QUAD):
        pairs = [(k, k // QUAD * QUAD + (k + d) % QUAD) for k in range(NZ)]
        parts.append((QUAD - d, lax.ppermute(share, COL, pairs)))
    for offset, part in parts:
        whole = lax.dynamic_update_index_in_dim(whole, part, lax.rem(place + offset, QUAD), 0)
    return whole


def spread(share, axes, size):
    return lax.all_to_all(jnp.broadcast_to(share[None], (size,) + share.shape), axes, 0, 0)


def sum_over_rows(rows, left, by_row):
    place = lax.rem(lax.axis_index(COL), QUAD)
    part = KV // QUAD
    columns = lax.dynamic_slice_in_dim(rows, place * part, part, 1)
    partial = dot(columns, left, ((0,), (0,)))
    share = lax.all_to_all(partial.reshape(NX * NY, -1, RANK), ("x", "row"), 0, 0)
    share = jnp.sum(share, axis=0)
    if not by_row:
        share = share_quad(share)
        whole = spread(share, ("x", "row"), NX * NY)
        return jnp.swapaxes(whole, 0, 1).reshape(KV, RANK)
    share = spread(share, ("x", "place"), NX * QUAD)
    whole = spread(share, "row", NY).reshape(NY, NX, QUAD, -1, RANK)
    return whole.transpose(2, 1, 0, 3, 4).reshape(KV, RANK)


def gather_rows(grad, momentum):
    core, x, z = (lax.axis_index(name) for name in ("core", "x", COL))
    pick = lambda array, m: lax.dynamic_index_in_dim(array[0], m, 0, False)
    buffer = lambda m: pick(momentum, m) + pick(grad, m).astype(jnp.float32)

    came = lax.ppermute(buffer(1 - core), "core", [(0, 1), (1, 0)])
    pieces = (buffer(core) + came).reshape(NX, -1, WIDTH)
    piece = lambda d: lax.dynamic_index_in_dim(pieces, lax.rem(x + d, NX), 0, False)
    came = [lax.ppermute(piece(d), "x", ring(NX, d)) for d in (2, 1, 3)]
    block = (piece(0) + came[1] + came[2] + came[0]) / (NX * NC)

    up, down = ring(NZ, 1), ring(NZ, -1)
    below = above = block
    parts = []
    for step in range(1, NZ // 2 + 1):
        below = lax.ppermute(below, COL, up)
        parts.append((NZ - step, below))
        if step < NZ // 2:
            above = lax.ppermute(above, COL, down)
            parts.append((step, above))
        if step == 1:
            parts.append((0, block))
    rows = jnp.zeros((block.shape[0], KV), jnp.float32)
    for offset, part in parts:
        rows = lax.dynamic_update_slice(rows, part, (0, lax.rem(z + offset, NZ) * WIDTH))
    return rows


def shards(grad, momentum, right_factor):
    core = lax.axis_index("core")
    own_factor = lax.dynamic_index_in_dim(right_factor, core, 1, False)
    own_factor, momentum, grad = lax.optimization_barrier((own_factor, momentum, grad))
    factor = lax.all_gather(own_factor, COL, axis=0, tiled=True)
    rows = gather_rows(grad, momentum)

    for repeat in range(ITERS):
        left = dot(rows, factor, ((1,), (0,)))
        product = sum_over_rows(rows, left, by_row=repeat == ITERS - 1)
        if repeat < ITERS - 1:
            factor = next_factor(product, factor)
    lefts = lax.all_gather(left, ("x", "core"), axis=0)

    sent = last_factor(lax.axis_index(COL), product, factor)
    got = lax.ppermute(sent, "core", [(0, 1), (1, 0)])
    return tuple(outputs(core, lefts, sent, got, momentum, grad))


def solution(mesh):
    shape = (NX, NC, NY, NZ // QUAD, QUAD)
    split = Mesh(mesh.devices.reshape(shape), ("x", "core", "row") + COL)
    data = P(("x", "core"), None, "row", COL)
    return jax.shard_map(
        shards,
        mesh=split,
        in_specs=(data, data, P(COL, None, None)),
        out_specs=(data, P(None, "row", COL), P(COL, None, None)),
        check_vma=False,
    )
```

```python
import math

import jax
import jax.numpy as jnp
from jax import lax
from jax.experimental import pallas as pl
from jax.experimental.pallas import tpu as pltpu
from jax.sharding import Mesh, PartitionSpec as P

D = 8192
KV = 1024
RANK = 256
ITERS = 2
NX, NC, NY, NZ = 4, 2, 4, 8
COL = ("quad", "place")
BLOCK = 64
PANEL = 16
QUAD = 4
WIDTH = KV // NZ

epsilon = 1e-06
decay_keep = 0.1
highest = lax.Precision.HIGHEST


def dot(a, b, contract):
    return lax.dot_general(
        a, b, (contract, ((), ())), precision=highest, preferred_element_type=jnp.float32
    )


def small_inverse_factor(block):
    size = block.shape[0]
    count = size // 8
    chunks = [block[8 * c : 8 * c + 8] for c in range(count)]
    sub = lax.broadcasted_iota(jnp.int32, (8, size), 0)
    lane = lax.broadcasted_iota(jnp.int32, (8, size), 1)
    pivots = [None] * count
    for lo in range(0, size, PANEL):
        spread = {}
        for c in range(lo // 8, count):
            for k in range(PANEL):
                spread[k, c] = jnp.broadcast_to(chunks[c][:, lo + k : lo + k + 1], (8, size))
        panel = (lane >= lo) & (lane < lo + PANEL)
        for c in range(lo // 8, count):
            unit = jnp.where(lane == sub + 8 * c, 1.0, 0.0) if 8 * c < lo + PANEL else 0.0
            chunks[c] = jnp.where(panel, unit, chunks[c])
        for j in range(PANEL):
            p, row = divmod(lo + j, 8)
            pivot = jnp.broadcast_to(spread[j, p][row : row + 1, :], (8, size))
            pivots[p] = jnp.where(sub >= row, pivot, pivot if row == 0 else pivots[p])
            scale = pltpu.reciprocal(pivot, approx=True)
            head = jnp.broadcast_to(chunks[p][row : row + 1, :], (8, size)) * scale
            heads = {
                k: jnp.broadcast_to(spread[k, p][row : row + 1, :], (8, size)) * scale
                for k in range(j + 1, PANEL)
            }
            for c in range(p, count):
                column = spread[j, c]
                if c == p:
                    column = jnp.where(sub > row, column, 0.0)
                chunks[c] = chunks[c] - column * head
                for k in heads:
                    spread[k, c] = spread[k, c] - column * heads[k]
    inverse = jnp.concatenate([c * lax.rsqrt(d) for c, d in zip(chunks, pivots)], axis=0)
    row_ids = lax.broadcasted_iota(jnp.int32, (size, size), 0)
    col_ids = lax.broadcasted_iota(jnp.int32, (size, size), 1)
    return jnp.where(col_ids <= row_ids, inverse, 0.0)


def inverse_factor(gram, out_ref):
    out_ref[...] = gram
    for lo in range(0, RANK, BLOCK):
        hi = lo + BLOCK
        rows = out_ref[lo:hi, :]
        inverse = small_inverse_factor(rows[:, lo:hi])
        scaled = dot(inverse, rows, ((1,), (0,)))
        parts = [scaled[:, :lo]] if lo else []
        parts.append(inverse)
        if hi < RANK:
            parts.append(scaled[:, hi:])
        pivot_rows = jnp.concatenate(parts, axis=1)
        if hi < RANK:
            update = dot(scaled[:, hi:], pivot_rows, ((0,), (0,)))
            below = out_ref[hi:, :]
            cols = lax.broadcasted_iota(jnp.int32, below.shape, 1)
            out_ref[hi:, :] = jnp.where((cols >= lo) & (cols < hi), 0.0, below) - update
        cols = lax.broadcasted_iota(jnp.int32, pivot_rows.shape, 1)
        out_ref[lo:hi, :] = jnp.where(cols < hi, pivot_rows, 0.0)


def orthonormal_right(product_ref, factor_ref, inverse_ref, right_ref):
    step = 2 * RANK
    chunk = lambda ref, c: ref[pl.ds(pl.multiple_of(c * step, step), step), :]
    zero = jnp.zeros((RANK, RANK), jnp.float32)
    add = lambda c, gram: gram + dot(chunk(factor_ref, c), chunk(product_ref, c), ((0,), (0,)))
    inverse_factor(lax.fori_loop(0, KV // step, add, zero), inverse_ref)

    def scale(c, squares):
        right = dot(chunk(product_ref, c), inverse_ref[...], ((1,), (1,)))
        right_ref[pl.ds(pl.multiple_of(c * step, step), step), :] = right
        return squares + jnp.sum(right * right, axis=0, keepdims=True)

    squares = lax.fori_loop(0, KV // step, scale, jnp.zeros((1, RANK), jnp.float32))
    return jnp.sqrt(squares + epsilon)


def next_factor_kernel(product_ref, factor_ref, out_ref, inverse_ref):
    norms = orthonormal_right(product_ref, factor_ref, inverse_ref, out_ref)
    out_ref[...] = out_ref[...] / norms


def last_factor_kernel(col_ref, product_ref, factor_ref, out_ref, inverse_ref, right_ref):
    norms = orthonormal_right(product_ref, factor_ref, inverse_ref, right_ref)
    right = right_ref[pl.ds(pl.multiple_of(col_ref[0] * WIDTH, WIDTH), WIDTH), :]
    factor = right / norms
    scale = math.sqrt(D * KV / RANK)
    stacked = jnp.concatenate([decay_keep * right, scale * factor], axis=0)
    out_ref[:RANK, :] = dot(stacked, inverse_ref[...], ((1,), (0,))).T
    out_ref[RANK:, :] = factor


vmem = pltpu.CompilerParams(vmem_limit_bytes=32 * 2**20)


def next_factor(product, factor):
    return pl.pallas_call(
        next_factor_kernel,
        out_shape=jax.ShapeDtypeStruct((KV, RANK), jnp.float32),
        scratch_shapes=[pltpu.VMEM((RANK, RANK), jnp.float32)],
        compiler_params=vmem,
        name="next_factor",
    )(product, factor)


def last_factor(col, product, factor):
    whole = pl.BlockSpec(memory_space=pltpu.VMEM)
    return pl.pallas_call(
        last_factor_kernel,
        in_specs=[pl.BlockSpec(memory_space=pltpu.SMEM), whole, whole],
        out_shape=jax.ShapeDtypeStruct((RANK + WIDTH, RANK), jnp.float32),
        scratch_shapes=[
            pltpu.VMEM((RANK, RANK), jnp.float32),
            pltpu.VMEM((KV, RANK), jnp.float32),
        ],
        compiler_params=vmem,
        name="last_factor",
    )(col[None], product, factor)


def halves(value):
    high = value.astype(jnp.bfloat16)
    return high, (value - high.astype(jnp.float32)).astype(jnp.bfloat16)


def output_kernel(
    core_ref, left_ref, own_ref, got_ref, momentum_ref, grad_ref,
    momentum_out, update_out, factor_out,
):
    matrix = pl.program_id(0)
    weight = jnp.where(matrix == core_ref[0], own_ref[:RANK, :], got_ref[:RANK, :])
    high, low = halves(weight)
    product = lambda a, b: jnp.dot(a, b, preferred_element_type=jnp.float32)
    rows = left_ref.shape[2]
    for x in range(NX):
        left_high, left_low = halves(left_ref[x, 0])
        both = product(left_low, high) + product(left_high, low) + product(left_high, high)
        here = slice(x * rows, (x + 1) * rows)
        buffer = momentum_ref[0, 0, here] + grad_ref[0, 0, here].astype(jnp.float32)
        momentum_out[0, 0, here] = buffer - both[:, :WIDTH]
        update_out[0, here] = both[:, WIDTH:].astype(jnp.bfloat16)

    @pl.when(matrix == 0)
    def _():
        first = core_ref[0] == 0
        mine, other = own_ref[RANK:, :], got_ref[RANK:, :]
        factor_out[:, 0, :] = jnp.where(first, mine, other)
        factor_out[:, 1, :] = jnp.where(first, other, mine)


def outputs(core, lefts, own, got, momentum, grad):
    rows = momentum.shape[2]
    data = pl.BlockSpec((1, 1, rows, WIDTH), lambda m: (0, m, 0, 0))
    weight = pl.BlockSpec((RANK + WIDTH, RANK), lambda m: (0, 0))
    return pl.pallas_call(
        output_kernel,
        grid=(NC,),
        in_specs=[
            pl.BlockSpec(memory_space=pltpu.SMEM),
            pl.BlockSpec((NX, 1, rows // NX, RANK), lambda m: (0, m, 0, 0)),
            weight,
            weight,
            data,
            data,
        ],
        out_specs=[
            data,
            pl.BlockSpec((1, rows, WIDTH), lambda m: (m, 0, 0)),
            pl.BlockSpec((WIDTH, NC, RANK), lambda m: (0, 0, 0)),
        ],
        out_shape=[
            jax.ShapeDtypeStruct(momentum.shape, jnp.float32),
            jax.ShapeDtypeStruct(momentum.shape[1:], jnp.bfloat16),
            jax.ShapeDtypeStruct((WIDTH, NC, RANK), jnp.float32),
        ],
        compiler_params=pltpu.CompilerParams(vmem_limit_bytes=56 * 2**20),
        name="outputs",
    )(core[None], lefts.reshape(NX, NC, -1, RANK), own, got, momentum, grad)


def ring(size, step):
    return [(k, (k + step) % size) for k in range(size)]


def share_quad(share):
    place = lax.rem(lax.axis_index(COL), QUAD)
    whole = jnp.broadcast_to(share[None], (QUAD,) + share.shape)
    parts = []
    for d in range(1, QUAD):
        pairs = [(k, k // QUAD * QUAD + (k + d) % QUAD) for k in range(NZ)]
        parts.append((QUAD - d, lax.ppermute(share, COL, pairs)))
    for offset, part in parts:
        whole = lax.dynamic_update_index_in_dim(whole, part, lax.rem(place + offset, QUAD), 0)
    return whole


def spread(share, axes, size):
    return lax.all_to_all(jnp.broadcast_to(share[None], (size,) + share.shape), axes, 0, 0)


def sum_over_rows(rows, left, by_row):
    place = lax.rem(lax.axis_index(COL), QUAD)
    part = KV // QUAD
    columns = lax.dynamic_slice_in_dim(rows, place * part, part, 1)
    partial = dot(columns, left, ((0,), (0,)))
    share = lax.all_to_all(partial.reshape(NX * NY, -1, RANK), ("x", "row"), 0, 0)
    share = jnp.sum(share, axis=0)
    if not by_row:
        share = share_quad(share)
        whole = spread(share, ("x", "row"), NX * NY)
        return jnp.swapaxes(whole, 0, 1).reshape(KV, RANK)
    share = spread(share, ("x", "place"), NX * QUAD)
    whole = spread(share, "row", NY).reshape(NY, NX, QUAD, -1, RANK)
    return whole.transpose(2, 1, 0, 3, 4).reshape(KV, RANK)


def gather_rows(grad, momentum):
    core, x, z = (lax.axis_index(name) for name in ("core", "x", COL))
    pick = lambda array, m: lax.dynamic_index_in_dim(array[0], m, 0, False)
    buffer = lambda m: pick(momentum, m) + pick(grad, m).astype(jnp.float32)

    came = lax.ppermute(buffer(1 - core), "core", [(0, 1), (1, 0)])
    pieces = (buffer(core) + came).reshape(NX, -1, WIDTH)
    piece = lambda d: lax.dynamic_index_in_dim(pieces, lax.rem(x + d, NX), 0, False)
    came = [lax.ppermute(piece(d), "x", ring(NX, d)) for d in (2, 1, 3)]
    block = (piece(0) + came[1] + came[2] + came[0]) / (NX * NC)

    up, down = ring(NZ, 1), ring(NZ, -1)
    below = above = block
    parts = []
    for step in range(1, NZ // 2 + 1):
        below = lax.ppermute(below, COL, up)
        parts.append((NZ - step, below))
        if step < NZ // 2:
            above = lax.ppermute(above, COL, down)
            parts.append((step, above))
        if step == 1:
            parts.append((0, block))
    rows = jnp.zeros((block.shape[0], KV), jnp.float32)
    for offset, part in parts:
        rows = lax.dynamic_update_slice(rows, part, (0, lax.rem(z + offset, NZ) * WIDTH))
    return rows


def shards(grad, momentum, right_factor):
    core = lax.axis_index("core")
    own_factor = lax.dynamic_index_in_dim(right_factor, core, 1, False)
    own_factor, momentum, grad = lax.optimization_barrier((own_factor, momentum, grad))
    factor = lax.all_gather(own_factor, COL, axis=0, tiled=True)
    rows = gather_rows(grad, momentum)

    for repeat in range(ITERS):
        left = dot(rows, factor, ((1,), (0,)))
        product = sum_over_rows(rows, left, by_row=repeat == ITERS - 1)
        if repeat < ITERS - 1:
            factor = next_factor(product, factor)
    lefts = lax.all_gather(left, ("x", "core"), axis=0)

    sent = last_factor(lax.axis_index(COL), product, factor)
    got = lax.ppermute(sent, "core", [(0, 1), (1, 0)])
    return tuple(outputs(core, lefts, sent, got, momentum, grad))


def solution(mesh):
    shape = (NX, NC, NY, NZ // QUAD, QUAD)
    split = Mesh(mesh.devices.reshape(shape), ("x", "core", "row") + COL)
    data = P(("x", "core"), None, "row", COL)
    return jax.shard_map(
        shards,
        mesh=split,
        in_specs=(data, data, P(COL, None, None)),
        out_specs=(data, P(None, "row", COL), P(COL, None, None)),
        check_vma=False,
    )
```
